512 devices in a mesh: tm: 32 (over y_hi, x, core), feat: 16 (over z, y_lo).
Axes of the slice: x: 4, y: 8 (y_hi: 4, y_lo: 2; y = y_hi * 2 + y_lo), z: 8, core: 2. Of those that a mesh axis runs over, the one named last changes fastest.
Arguments:
- frames: float32 [8192, 8192], P('tm', 'feat'), as said below
Outputs:
- cov_instant: float32 [8192, 8192], P('feat', 'tm')
- cov_lagged: float32 [8192, 8192], P('feat', 'tm')
- cov_later: float32 [8192, 8192], P('feat', 'tm')
Inputs may be any that keep to these rules, and one draw needn't show every extreme that they name: `frames`: real-valued features of a molecular trajectory; entries are of order one to some tens.
All inputs are finite; a program needn't handle non-finite values.
Results may differ from the reference program's by a relative error of at most 0.00051.
Values may be sent and summed in bfloat16 or wider, within the bound.
A program may use at most 64 MiB of HBM per device.

```python
import jax
import jax.numpy as jnp
from jax import lax

F = 8192
LAG = 256
NF = 8192


def draw_frames(key, part):
    key = jax.random.fold_in(key, 11)
    key_scale, key_drift, key_couple, key_noise = jax.random.split(key, 4)
    scales = jnp.exp(jax.random.uniform(key_scale, (F,), jnp.float32, jnp.log(0.3), jnp.log(3.0)))
    drifts = 1.5 * jax.random.normal(key_drift, (F,), jnp.float32)
    coupling = jax.random.uniform(key_couple, (F,), jnp.float32, 0.3, 0.9)
    noise = jax.random.normal(key_noise, (NF + LAG, F), jnp.float32)
    recent = noise[LAG:]
    earlier = noise[:NF]
    mixed = recent + 0.6 * jnp.roll(recent, 1, axis=1) + coupling * jnp.roll(earlier, 37, axis=1)
    growth = 1.0 + 2.0 * jnp.arange(NF, dtype=jnp.float32) / NF
    return scales * mixed + drifts * growth[:, None]


def setup_inputs(seed: int = 0) -> dict:
    arg_keys = jax.random.split(jax.random.key(seed), 2)
    return {
        "frames": draw_frames(jax.random.fold_in(arg_keys[1], 71), 0),
    }


def reference(frames):
    kept_frames = NF - LAG
    frame_mean = jnp.sum(frames, axis=0) / NF
    centred = (frames - frame_mean).astype(jnp.bfloat16)
    head = centred[:kept_frames].astype(jnp.float32)
    tail = centred[LAG:].astype(jnp.float32)
    contract = (((0,), (0,)), ((), ()))
    cov_instant = lax.dot_general(head, head, contract, precision=lax.Precision.HIGHEST, preferred_element_type=jnp.float32) / kept_frames
    cov_lagged = lax.dot_general(head, tail, contract, precision=lax.Precision.HIGHEST, preferred_element_type=jnp.float32) / kept_frames
    cov_later = lax.dot_general(tail, tail, contract, precision=lax.Precision.HIGHEST, preferred_element_type=jnp.float32) / kept_frames
    return (cov_instant, cov_lagged, cov_later)
```

```python
import functools

import jax
import jax.numpy as jnp
from jax import lax
from jax.experimental import pallas as pl
from jax.experimental.pallas import tpu as pltpu
from jax.sharding import PartitionSpec as P

LAG = 256
MESH = pl.DeviceIdType.MESH

NYH, NX, NZ = 4, 4, 8
NT = NYH * NX
N_COPIES = 80


def mod(a, n):
    return lax.rem(a + n, n)


def kernel(
    x_hbm, inst, lagged, later, xv, halves, pair, sums, rows, cols, in_sem, send_sem, recv_sem, turn_sem
):
    tm = lax.axis_index("tm")
    feat = lax.axis_index("feat")
    c = lax.rem(tm, 2)
    t = tm // 2
    yh, x = t // NX, lax.rem(t, NX)
    z, yl = feat // 2, lax.rem(feat, 2)
    p = feat
    diagonal = t == p

    def device(dyh=0, dx=0, dz=0, core=c, yl=yl):
        return {
            "tm": (mod(yh + dyh, NYH) * NX + mod(x + dx, NX)) * 2 + core,
            "feat": mod(z + dz, NZ) * 2 + yl,
        }

    peers = [(a, b) for a in range(NYH) for b in range(NX) if a or b]

    barrier = pltpu.get_barrier_semaphore()
    load = pltpu.make_async_copy(x_hbm, xv, in_sem)
    load.start()
    near = [device(core=1 - c), device(dz=1), device(dz=-1), device(yl=1 - yl)]
    near += [device(dyh=a, dx=b) for a, b in peers]
    for who in near:
        pl.semaphore_signal(barrier, inc=1, device_id=who, device_id_type=MESH)

    @pl.when(jnp.logical_not(diagonal))
    def _():
        for h in range(2):
            pl.semaphore_signal(
                barrier, inc=1, device_id={"tm": 2 * p + h, "feat": t}, device_id_type=MESH
            )

    load.wait()
    column_sums = jnp.sum(xv[...], axis=0, keepdims=True)
    for k in range(4):
        pair[0, k : k + 1, :] = column_sums[:, 128 * k : 128 * (k + 1)]
        pair[0, 4 + k : 5 + k, :] = column_sums[:, 128 * k : 128 * (k + 1)]
    pl.semaphore_wait(barrier, len(near) + 2 * (1 - diagonal.astype(jnp.int32)))

    sent = []

    def send(src, dst, who):
        k = len(sent)
        copy = pltpu.make_async_remote_copy(
            src_ref=src,
            dst_ref=dst,
            send_sem=send_sem.at[k],
            recv_sem=recv_sem.at[k],
            device_id=who,
            device_id_type=MESH,
        )
        copy.start()
        sent.append(copy)
        return copy

    send(pair.at[0], pair.at[1], device(core=1 - c)).wait_recv()
    sums[t] = pair[0] + pair[1]
    arrivals = [send(sums.at[t], sums.at[t], device(dyh=a, dx=b)) for a, b in peers]
    for copy in arrivals:
        copy.wait_recv()
    total = sums[0]
    for k in range(1, NT):
        total = total + sums[k]
    mean = total / (LAG * 2 * NT)

    lanes = pl.ds(pl.multiple_of(c * LAG, LAG), LAG)
    for k in range(4):
        part = (xv[:, 128 * k : 128 * (k + 1)] - mean[k : k + 1, :]).astype(jnp.bfloat16)
        halves[k // 2, :, 128 * (k % 2) : 128 * (k % 2 + 1)] = part
        rows[t, 128 * k : 128 * (k + 1), lanes] = part.T

    def row(dyh, dx, half=None):
        s = mod(yh + dyh, NYH) * NX + mod(x + dx, NX)
        if half is None:
            return rows.at[s, :, lanes]
        return rows.at[s, pl.ds(256 * half, 256), lanes]

    def col(dz, side, half=None):
        s = mod(z + dz, NZ) * 2 + side
        if half is None:
            return cols.at[pl.ds(pl.multiple_of(s * 512, 512), 512), :]
        return cols.at[pl.ds(pl.multiple_of(s * 512 + 256 * half, 256), 256), :]

    def turned(half):
        return cols.at[pl.ds(pl.multiple_of(t * 512 + half * 256, 256), 256), :]

    for h in range(2):
        itself = jnp.logical_and(diagonal, c == h)
        copy = pltpu.make_async_remote_copy(
            src_ref=halves.at[h],
            dst_ref=turned(c),
            send_sem=turn_sem.at[h],
            recv_sem=turn_sem.at[2 + c],
            device_id={"tm": 2 * p + h, "feat": t},
            device_id_type=MESH,
        )
        local = pltpu.make_async_copy(halves.at[h], turned(c), turn_sem.at[2 + c])

        @pl.when(itself)
        def _():
            local.start()

        @pl.when(jnp.logical_not(itself))
        def _():
            copy.start()

    def both(dyh, dx):
        return (
            send(row(dyh, dx), row(dyh, dx), device(dx=1)),
            send(row(dyh, dx), row(dyh, dx), device(dx=-1)),
        )

    def far_x(dyh):
        return (
            send(row(dyh, -1, 0), row(dyh, -1, 0), device(dx=1)),
            send(row(dyh, 1, 1), row(dyh, 1, 1), device(dx=-1)),
        )

    twins = []

    def twin(dyh, dx):
        twins.append(send(row(dyh, dx), row(dyh, dx), device(core=1 - c)))

    def wait(copies):
        for copy in copies:
            copy.wait_recv()

    def z_both(plus, minus, side, halved=False):
        a, b = (0, 1) if halved else (None, None)
        return (
            send(col(plus, side, a), col(plus, side, a), device(dz=1)),
            send(col(minus, side, b), col(minus, side, b), device(dz=-1)),
        )

    y_near = (
        send(row(0, 0), row(0, 0), device(dyh=1)),
        send(row(0, 0), row(0, 0), device(dyh=-1)),
    )
    x_own = both(0, 0)
    twin(0, 0)

    for h in range(2):
        pltpu.make_async_copy(halves.at[h], col(0, yl, h), turn_sem.at[2 + h]).wait()
    own1 = z_both(0, 0, yl)
    cross0 = send(col(0, yl), col(0, yl), device(yl=1 - yl))

    wait(x_own)
    x_own_far = far_x(0)
    twin(0, -1)
    twin(0, 1)

    wait(own1)
    own2 = z_both(-1, 1, yl)
    cross1 = send(col(-1, yl), col(-1, yl), device(yl=1 - yl))
    wait([cross0])
    other1m = send(col(0, 1 - yl), col(0, 1 - yl), device(dz=-1))

    wait(y_near)
    y_far = (
        send(row(-1, 0, 0), row(-1, 0, 0), device(dyh=1)),
        send(row(1, 0, 1), row(1, 0, 1), device(dyh=-1)),
    )
    x_before = both(-1, 0)
    x_after = both(1, 0)
    twin(-1, 0)
    twin(1, 0)
    wait(x_own_far)
    twin(0, 2)

    wait([cross1])
    other1p = send(col(-1, 1 - yl), col(-1, 1 - yl), device(dz=1))
    wait(own2)
    own3 = z_both(-2, 2, yl)

    wait(x_before)
    x_before_far = far_x(-1)
    twin(-1, -1)
    twin(-1, 1)
    wait(y_far)
    x_last = both(2, 0)
    twin(2, 0)

    wait([other1m, other1p])
    other2 = z_both(-2, 1, 1 - yl)

    wait(x_after)
    x_after_far = far_x(1)
    twin(1, -1)
    twin(1, 1)
    wait(own3)
    own4 = z_both(-3, 3, yl, halved=True)
    wait(x_before_far)
    twin(-1, 2)
    wait(other2)
    other3 = z_both(-3, 2, 1 - yl)
    wait(x_last)
    x_last_far = far_x(2)
    twin(2, -1)
    twin(2, 1)
    wait(x_after_far)
    twin(1, 2)
    wait(x_last_far)
    twin(2, 2)
    wait(own4)
    wait(other3)
    wait(twins)

    def product(lhs, rhs):
        return jnp.dot(lhs, rhs, preferred_element_type=jnp.float32)

    kept = LAG * (2 * NT - 1)
    inst[...] = product(rows[0, :, LAG:], cols[LAG : 2 * LAG, :])
    lagged[...] = product(rows[0], cols[LAG : 3 * LAG, :])

    @pl.loop(1, NT - 1)
    def _(s):
        inst[...] += product(rows[s], cols[pl.ds(pl.multiple_of(s * 512, 512), 512), :])
        lagged[...] += product(rows[s], cols[pl.ds(pl.multiple_of(s * 512 + 256, 256), 512), :])

    last = NT - 1
    head = rows[last, :, :LAG]
    middle = inst[...] + product(head, cols[512 * last : 512 * last + LAG, :])
    lagged[...] = (lagged[...] + product(head, cols[512 * last + LAG :, :])) / kept
    inst[...] = (middle + product(rows[0, :, :LAG], cols[:LAG, :])) / kept
    later[...] = (middle + product(rows[last, :, LAG:], cols[512 * last + LAG :, :])) / kept

    for copy in sent:
        copy.wait_send()
    for h in range(2):

        @pl.when(jnp.logical_not(jnp.logical_and(diagonal, c == h)))
        def _():
            pltpu.make_async_copy(halves.at[h], halves.at[h], turn_sem.at[h]).wait()


def on_device(frames):
    frame_count, panel = frames.shape
    block = jax.ShapeDtypeStruct((panel, frame_count), jnp.float32)
    vmem = pl.BlockSpec(memory_space=pltpu.VMEM)
    return pl.pallas_call(
        kernel,
        out_shape=(block, block, block),
        in_specs=[pl.BlockSpec(memory_space=pl.ANY)],
        out_specs=(vmem, vmem, vmem),
        scratch_shapes=[
            pltpu.VMEM((frame_count, panel), jnp.float32),
            pltpu.VMEM((2, frame_count, panel // 2), jnp.bfloat16),
            pltpu.VMEM((2, 8, 128), jnp.float32),
            pltpu.VMEM((NT, 8, 128), jnp.float32),
            pltpu.VMEM((NT, panel, 2 * frame_count), jnp.bfloat16),
            pltpu.VMEM((NT * 2 * frame_count, panel // 2), jnp.bfloat16),
            pltpu.SemaphoreType.DMA,
            pltpu.SemaphoreType.DMA((N_COPIES,)),
            pltpu.SemaphoreType.DMA((N_COPIES,)),
            pltpu.SemaphoreType.DMA((4,)),
        ],
        compiler_params=pltpu.CompilerParams(
            collective_id=0, has_side_effects=True, vmem_limit_bytes=40 * 1024 * 1024
        ),
        cost_estimate=pl.CostEstimate(
            flops=4 * panel * frame_count * 8192, bytes_accessed=1 << 21, transcendentals=0
        ),
    )(frames)


def solution(mesh):
    return jax.shard_map(
        on_device,
        mesh=mesh,
        in_specs=(P("tm", "feat"),),
        out_specs=(P("feat", "tm"), P("feat", "tm"), P("feat", "tm")),
        check_vma=False,
    )
```

```python
import functools

import jax
import jax.numpy as jnp
from jax import lax
from jax.experimental import pallas as pl
from jax.experimental.pallas import tpu as pltpu
from jax.sharding import PartitionSpec as P

LAG = 256
MESH = pl.DeviceIdType.MESH

NYH, NX, NZ = 4, 4, 8
NT = NYH * NX
N_COPIES = 80


def mod(a, n):
    return lax.rem(a + n, n)


def kernel(
    x_hbm, inst, lagged, later, xv, halves, passing, pair, sums, rows, cols, in_sem, send_sem, recv_sem, turn_sem
):
    tm = lax.axis_index("tm")
    feat = lax.axis_index("feat")
    c = lax.rem(tm, 2)
    t = tm // 2
    yh, x = t // NX, lax.rem(t, NX)
    z, yl = feat // 2, lax.rem(feat, 2)
    p = feat
    plane = mod(x // 2 - 2 * yh - z + NZ, NZ)
    passed = 2 * plane + yl

    def block_at(z, side):
        shift = t // 2 + z
        high = lax.rem(shift, 2)
        return mod(high - shift + 2 * NZ, NZ) // 2 * NX + 2 * high + side

    mine = block_at(z, yl)
    in_plane = plane == z
    stays = jnp.logical_and(passed == t, mine == t)

    def device(dyh=0, dx=0, dz=0, core=c, yl=yl):
        return {
            "tm": (mod(yh + dyh, NYH) * NX + mod(x + dx, NX)) * 2 + core,
            "feat": mod(z + dz, NZ) * 2 + yl,
        }

    peers = [(a, b) for a in range(NYH) for b in range(NX) if a or b]

    barrier = pltpu.get_barrier_semaphore()
    load = pltpu.make_async_copy(x_hbm, xv, in_sem)
    load.start()
    near = [device(core=1 - c), device(dz=1), device(dz=-1), device(yl=1 - yl)]
    near += [device(dyh=a, dx=b) for a, b in peers]
    for who in near:
        pl.semaphore_signal(barrier, inc=1, device_id=who, device_id_type=MESH)

    @pl.when(jnp.logical_not(stays))
    def _():
        for h in range(2):
            pl.semaphore_signal(
                barrier, inc=1, device_id={"tm": 2 * mine + h, "feat": 2 * z + lax.rem(x, 2)}, device_id_type=MESH
            )

    mirror = {"tm": tm, "feat": 2 * plane + yl}

    @pl.when(jnp.logical_not(in_plane))
    def _():
        pl.semaphore_signal(barrier, inc=1, device_id=mirror, device_id_type=MESH)

    load.wait()
    column_sums = jnp.sum(xv[...], axis=0, keepdims=True)
    for k in range(4):
        pair[0, k : k + 1, :] = column_sums[:, 128 * k : 128 * (k + 1)]
        pair[0, 4 + k : 5 + k, :] = column_sums[:, 128 * k : 128 * (k + 1)]
    pl.semaphore_wait(barrier, len(near) + 3 - 2 * stays.astype(jnp.int32) - in_plane.astype(jnp.int32))

    sent = []

    def send(src, dst, who):
        k = len(sent)
        copy = pltpu.make_async_remote_copy(
            src_ref=src,
            dst_ref=dst,
            send_sem=send_sem.at[k],
            recv_sem=recv_sem.at[k],
            device_id=who,
            device_id_type=MESH,
        )
        copy.start()
        sent.append(copy)
        return copy

    send(pair.at[0], pair.at[1], device(core=1 - c)).wait_recv()
    sums[t] = pair[0] + pair[1]
    arrivals = [send(sums.at[t], sums.at[t], device(dyh=a, dx=b)) for a, b in peers]
    for copy in arrivals:
        copy.wait_recv()
    total = sums[0]
    for k in range(1, NT):
        total = total + sums[k]
    mean = total / (LAG * 2 * NT)

    lanes = pl.ds(pl.multiple_of(c * LAG, LAG), LAG)
    for k in range(4):
        part = (xv[:, 128 * k : 128 * (k + 1)] - mean[k : k + 1, :]).astype(jnp.bfloat16)
        halves[k // 2, :, 128 * (k % 2) : 128 * (k % 2 + 1)] = part
        rows[t, 128 * k : 128 * (k + 1), lanes] = part.T

    def row(dyh, dx, half=None):
        s = mod(yh + dyh, NYH) * NX + mod(x + dx, NX)
        if half is None:
            return rows.at[s, :, lanes]
        return rows.at[s, pl.ds(256 * half, 256), lanes]

    def col(dz, side, half=None):
        s = block_at(mod(z + dz, NZ), side)
        if half is None:
            return cols.at[pl.ds(pl.multiple_of(s * 512, 512), 512), :]
        return cols.at[pl.ds(pl.multiple_of(s * 512 + 256 * half, 256), 256), :]

    def turned(half):
        return cols.at[pl.ds(pl.multiple_of(t * 512 + half * 256, 256), 256), :]

    for h in range(2):
        copy = pltpu.make_async_remote_copy(
            src_ref=halves.at[h],
            dst_ref=passing.at[h],
            send_sem=turn_sem.at[h],
            recv_sem=turn_sem.at[2 + h],
            device_id=mirror,
            device_id_type=MESH,
        )
        local = pltpu.make_async_copy(halves.at[h], passing.at[h], turn_sem.at[2 + h])

        @pl.when(in_plane)
        def _():
            local.start()

        @pl.when(jnp.logical_not(in_plane))
        def _():
            copy.start()

    def turn(h):
        itself = jnp.logical_and(stays, c == h)
        pltpu.make_async_copy(halves.at[h], passing.at[h], turn_sem.at[2 + h]).wait()
        copy = pltpu.make_async_remote_copy(
            src_ref=passing.at[h],
            dst_ref=turned(c),
            send_sem=turn_sem.at[4 + h],
            recv_sem=turn_sem.at[6 + c],
            device_id={"tm": 2 * passed + h, "feat": 2 * z + lax.rem(x, 2)},
            device_id_type=MESH,
        )
        local = pltpu.make_async_copy(passing.at[h], turned(c), turn_sem.at[6 + c])

        @pl.when(itself)
        def _():
            local.start()

        @pl.when(jnp.logical_not(itself))
        def _():
            copy.start()

    def both(dyh, dx):
        return (
            send(row(dyh, dx), row(dyh, dx), device(dx=1)),
            send(row(dyh, dx), row(dyh, dx), device(dx=-1)),
        )

    def far_x(dyh):
        return (
            send(row(dyh, -1, 0), row(dyh, -1, 0), device(dx=1)),
            send(row(dyh, 1, 1), row(dyh, 1, 1), device(dx=-1)),
        )

    twins = []

    def twin(dyh, dx):
        twins.append(send(row(dyh, dx), row(dyh, dx), device(core=1 - c)))

    def wait(copies):
        for copy in copies:
            copy.wait_recv()

    def z_both(plus, minus, side, halved=False):
        a, b = (0, 1) if halved else (None, None)
        return (
            send(col(plus, side, a), col(plus, side, a), device(dz=1)),
            send(col(minus, side, b), col(minus, side, b), device(dz=-1)),
        )

    y_near = (
        send(row(0, 0), row(0, 0), device(dyh=1)),
        send(row(0, 0), row(0, 0), device(dyh=-1)),
    )
    x_own = both(0, 0)
    twin(0, 0)

    turn(0)
    turn(1)
    for h in range(2):
        pltpu.make_async_copy(passing.at[h], col(0, yl, h), turn_sem.at[6 + h]).wait()
    own1 = z_both(0, 0, yl)
    cross0 = send(col(0, yl), col(0, yl), device(yl=1 - yl))

    wait(x_own)
    x_own_far = far_x(0)
    twin(0, -1)
    twin(0, 1)

    wait(own1)
    own2 = z_both(-1, 1, yl)
    cross1 = send(col(-1, yl), col(-1, yl), device(yl=1 - yl))
    wait([cross0])
    other1m = send(col(0, 1 - yl), col(0, 1 - yl), device(dz=-1))

    wait(y_near)
    y_far = (
        send(row(-1, 0, 0), row(-1, 0, 0), device(dyh=1)),
        send(row(1, 0, 1), row(1, 0, 1), device(dyh=-1)),
    )
    x_before = both(-1, 0)
    x_after = both(1, 0)
    twin(-1, 0)
    twin(1, 0)
    wait(x_own_far)
    twin(0, 2)

    wait([cross1])
    other1p = send(col(-1, 1 - yl), col(-1, 1 - yl), device(dz=1))
    wait(own2)
    own3 = z_both(-2, 2, yl)

    wait(x_before)
    x_before_far = far_x(-1)
    twin(-1, -1)
    twin(-1, 1)
    wait(y_far)
    x_last = both(2, 0)
    twin(2, 0)

    wait([other1m, other1p])
    other2 = z_both(-2, 1, 1 - yl)

    wait(x_after)
    x_after_far = far_x(1)
    twin(1, -1)
    twin(1, 1)
    wait(own3)
    own4 = z_both(-3, 3, yl, halved=True)
    wait(x_before_far)
    twin(-1, 2)
    wait(other2)
    other3 = z_both(-3, 2, 1 - yl)
    wait(x_last)
    x_last_far = far_x(2)
    twin(2, -1)
    twin(2, 1)
    wait(x_after_far)
    twin(1, 2)
    wait(x_last_far)
    twin(2, 2)
    wait(own4)
    wait(other3)
    wait(twins)

    def product(lhs, rhs):
        return jnp.dot(lhs, rhs, preferred_element_type=jnp.float32)

    kept = LAG * (2 * NT - 1)
    inst[...] = product(rows[0, :, LAG:], cols[LAG : 2 * LAG, :])
    lagged[...] = product(rows[0], cols[LAG : 3 * LAG, :])

    @pl.loop(1, NT - 1)
    def _(s):
        inst[...] += product(rows[s], cols[pl.ds(pl.multiple_of(s * 512, 512), 512), :])
        lagged[...] += product(rows[s], cols[pl.ds(pl.multiple_of(s * 512 + 256, 256), 512), :])

    last = NT - 1
    head = rows[last, :, :LAG]
    middle = inst[...] + product(head, cols[512 * last : 512 * last + LAG, :])
    lagged[...] = (lagged[...] + product(head, cols[512 * last + LAG :, :])) / kept
    inst[...] = (middle + product(rows[0, :, :LAG], cols[:LAG, :])) / kept
    later[...] = (middle + product(rows[last, :, LAG:], cols[512 * last + LAG :, :])) / kept

    for copy in sent:
        copy.wait_send()
    for h in range(2):

        @pl.when(jnp.logical_not(in_plane))
        def _():
            pltpu.make_async_copy(halves.at[h], halves.at[h], turn_sem.at[h]).wait()

        @pl.when(jnp.logical_not(jnp.logical_and(stays, c == h)))
        def _():
            pltpu.make_async_copy(passing.at[h], passing.at[h], turn_sem.at[4 + h]).wait()


def on_device(frames):
    frame_count, panel = frames.shape
    block = jax.ShapeDtypeStruct((panel, frame_count), jnp.float32)
    vmem = pl.BlockSpec(memory_space=pltpu.VMEM)
    return pl.pallas_call(
        kernel,
        out_shape=(block, block, block),
        in_specs=[pl.BlockSpec(memory_space=pl.ANY)],
        out_specs=(vmem, vmem, vmem),
        scratch_shapes=[
            pltpu.VMEM((frame_count, panel), jnp.float32),
            pltpu.VMEM((2, frame_count, panel // 2), jnp.bfloat16),
            pltpu.VMEM((2, frame_count, panel // 2), jnp.bfloat16),
            pltpu.VMEM((2, 8, 128), jnp.float32),
            pltpu.VMEM((NT, 8, 128), jnp.float32),
            pltpu.VMEM((NT, panel, 2 * frame_count), jnp.bfloat16),
            pltpu.VMEM((NT * 2 * frame_count, panel // 2), jnp.bfloat16),
            pltpu.SemaphoreType.DMA,
            pltpu.SemaphoreType.DMA((N_COPIES,)),
            pltpu.SemaphoreType.DMA((N_COPIES,)),
            pltpu.SemaphoreType.DMA((8,)),
        ],
        compiler_params=pltpu.CompilerParams(
            collective_id=0, has_side_effects=True, vmem_limit_bytes=40 * 1024 * 1024
        ),
        cost_estimate=pl.CostEstimate(
            flops=4 * panel * frame_count * 8192, bytes_accessed=1 << 21, transcendentals=0
        ),
    )(frames)


def solution(mesh):
    return jax.shard_map(
        on_device,
        mesh=mesh,
        in_specs=(P("tm", "feat"),),
        out_specs=(P("feat", "tm"), P("feat", "tm"), P("feat", "tm")),
        check_vma=False,
    )
```

```python
import functools

import jax
import jax.numpy as jnp
from jax import lax
from jax.experimental import pallas as pl
from jax.experimental.pallas import tpu as pltpu
from jax.sharding import PartitionSpec as P

LAG = 256
MESH = pl.DeviceIdType.MESH

NYH, NX, NZ = 4, 4, 8
NT = NYH * NX
N_COPIES = 80


def mod(a, n):
    return lax.rem(a + n, n)


def kernel(
    x_hbm, inst, lagged, later, xv, halves, passing, means, table, passing_table, other_table, middle, rows, cols, in_sem, send_sem, recv_sem, turn_sem
):
    tm = lax.axis_index("tm")
    feat = lax.axis_index("feat")
    c = lax.rem(tm, 2)
    t = tm // 2
    yh, x = t // NX, lax.rem(t, NX)
    z, yl = feat // 2, lax.rem(feat, 2)
    p = feat
    plane = mod(x // 2 - 2 * yh - z + NZ, NZ)
    passed = 2 * plane + yl

    def block_at(z, side):
        shift = t // 2 + z
        high = lax.rem(shift, 2)
        return mod(high - shift + 2 * NZ, NZ) // 2 * NX + 2 * high + side

    mine = block_at(z, yl)
    in_plane = plane == z
    stays = jnp.logical_and(passed == t, mine == t)

    def device(dyh=0, dx=0, dz=0, core=c, yl=yl):
        return {
            "tm": (mod(yh + dyh, NYH) * NX + mod(x + dx, NX)) * 2 + core,
            "feat": mod(z + dz, NZ) * 2 + yl,
        }

    peers = [(a, b) for a in range(NYH) for b in range(NX) if a or b]

    barrier = pltpu.get_barrier_semaphore()
    load = pltpu.make_async_copy(x_hbm, xv, in_sem)
    load.start()
    near = [device(core=1 - c), device(dz=1), device(dz=-1), device(yl=1 - yl)]
    near += [device(dyh=a, dx=b) for a, b in peers]
    for who in near:
        pl.semaphore_signal(barrier, inc=1, device_id=who, device_id_type=MESH)

    @pl.when(jnp.logical_not(stays))
    def _():
        for h in range(2):
            pl.semaphore_signal(
                barrier, inc=1, device_id={"tm": 2 * mine + h, "feat": 2 * z + lax.rem(x, 2)}, device_id_type=MESH
            )

    mirror = {"tm": tm, "feat": 2 * plane + yl}

    @pl.when(jnp.logical_not(in_plane))
    def _():
        pl.semaphore_signal(barrier, inc=1, device_id=mirror, device_id_type=MESH)

    load.wait()
    lanes = pl.ds(pl.multiple_of(c * LAG, LAG), LAG)
    block_mean = jnp.sum(xv[...], axis=0, keepdims=True) / LAG
    for k in range(4):
        mean = block_mean[:, 128 * k : 128 * (k + 1)]
        means[c, t, k : k + 1, :] = mean
        means[c, t, 4 + k : 5 + k, :] = mean
        part = (xv[:, 128 * k : 128 * (k + 1)] - mean).astype(jnp.bfloat16)
        halves[k // 2, :, 128 * (k % 2) : 128 * (k % 2 + 1)] = part
        rows[t, 128 * k : 128 * (k + 1), lanes] = part.T
    pl.semaphore_wait(barrier, len(near) + 3 - 2 * stays.astype(jnp.int32) - in_plane.astype(jnp.int32))

    sent = []

    def send(src, dst, who):
        k = len(sent)
        copy = pltpu.make_async_remote_copy(
            src_ref=src,
            dst_ref=dst,
            send_sem=send_sem.at[k],
            recv_sem=recv_sem.at[k],
            device_id=who,
            device_id_type=MESH,
        )
        copy.start()
        sent.append(copy)
        return copy

    def row(dyh, dx, half=None):
        s = mod(yh + dyh, NYH) * NX + mod(x + dx, NX)
        if half is None:
            return rows.at[s, :, lanes]
        return rows.at[s, pl.ds(256 * half, 256), lanes]

    def col(dz, side, half=None):
        s = block_at(mod(z + dz, NZ), side)
        if half is None:
            return cols.at[pl.ds(pl.multiple_of(s * 512, 512), 512), :]
        return cols.at[pl.ds(pl.multiple_of(s * 512 + 256 * half, 256), 256), :]

    def turned(half):
        return cols.at[pl.ds(pl.multiple_of(t * 512 + half * 256, 256), 256), :]

    def along_z(src, dst, k):
        copy = pltpu.make_async_remote_copy(
            src_ref=src,
            dst_ref=dst,
            send_sem=turn_sem.at[k],
            recv_sem=turn_sem.at[2 + k],
            device_id=mirror,
            device_id_type=MESH,
        )
        local = pltpu.make_async_copy(src, dst, turn_sem.at[2 + k])

        @pl.when(in_plane)
        def _():
            local.start()

        @pl.when(jnp.logical_not(in_plane))
        def _():
            copy.start()

    def within_plane(src, dst, h, send_k, recv_k):
        itself = jnp.logical_and(stays, c == h)
        copy = pltpu.make_async_remote_copy(
            src_ref=src,
            dst_ref=dst,
            send_sem=turn_sem.at[send_k],
            recv_sem=turn_sem.at[recv_k],
            device_id={"tm": 2 * passed + h, "feat": 2 * z + lax.rem(x, 2)},
            device_id_type=MESH,
        )
        local = pltpu.make_async_copy(src, dst, turn_sem.at[recv_k])

        @pl.when(itself)
        def _():
            local.start()

        @pl.when(jnp.logical_not(itself))
        def _():
            copy.start()

    def landed(ref, k):
        pltpu.make_async_copy(ref, ref, turn_sem.at[k]).wait()

    for h in range(2):
        along_z(halves.at[h], passing.at[h], h)

    def turn(h):
        landed(passing.at[h], 2 + h)
        within_plane(passing.at[h], turned(c), h, 4 + h, 6 + c)

    def both(dyh, dx):
        return (
            send(row(dyh, dx), row(dyh, dx), device(dx=1)),
            send(row(dyh, dx), row(dyh, dx), device(dx=-1)),
        )

    def far_x(dyh):
        return (
            send(row(dyh, -1, 0), row(dyh, -1, 0), device(dx=1)),
            send(row(dyh, 1, 1), row(dyh, 1, 1), device(dx=-1)),
        )

    twins = []

    def twin(dyh, dx):
        twins.append(send(row(dyh, dx), row(dyh, dx), device(core=1 - c)))

    def wait(copies):
        for copy in copies:
            copy.wait_recv()

    def z_both(plus, minus, side, halved=False):
        a, b = (0, 1) if halved else (None, None)
        return (
            send(col(plus, side, a), col(plus, side, a), device(dz=1)),
            send(col(minus, side, b), col(minus, side, b), device(dz=-1)),
        )

    def cross(dz):
        return send(col(dz, yl), col(dz, yl), device(yl=1 - yl))

    y_near = (
        send(row(0, 0), row(0, 0), device(dyh=1)),
        send(row(0, 0), row(0, 0), device(dyh=-1)),
    )
    x_own = both(0, 0)
    twin(0, 0)

    turn(0)
    turn(1)
    mean_arrivals = [send(means.at[c, t], means.at[c, t], device(dyh=a, dx=b)) for a, b in peers]
    for h in range(2):
        landed(passing.at[h], 6 + h)
    own1 = z_both(0, 0, yl)
    cross0 = cross(0)

    wait(x_own)
    x_own_far = far_x(0)
    twin(0, -1)
    twin(0, 1)

    wait(own1)
    own2 = z_both(-1, 1, yl)
    cross1 = (cross(-1), cross(1))

    wait(y_near)
    y_far = (
        send(row(-1, 0, 0), row(-1, 0, 0), device(dyh=1)),
        send(row(1, 0, 1), row(1, 0, 1), device(dyh=-1)),
    )
    x_before = both(-1, 0)
    x_after = both(1, 0)
    twin(-1, 0)
    twin(1, 0)
    wait(x_own_far)
    twin(0, 2)

    wait(mean_arrivals)
    mean_twin = send(means.at[c], means.at[c], device(core=1 - c))

    wait(own2)
    own3 = z_both(-2, 2, yl)
    wait([mean_twin])
    for s in range(NT):
        for core in range(2):
            for k in range(4):
                line = 2 * s + core
                table[k // 2, line : line + 1, 128 * (k % 2) : 128 * (k % 2 + 1)] = means[core, s, k : k + 1, :]

    along_z(table.at[c], passing_table, 8)

    wait(x_before)
    x_before_far = far_x(-1)
    twin(-1, -1)
    twin(-1, 1)
    wait([cross0])
    wait(cross1)
    other1 = z_both(-1, 1, 1 - yl)
    wait(y_far)
    x_last = both(2, 0)
    twin(2, 0)

    wait(own3)
    own4 = z_both(-3, 3, yl, halved=True)

    wait(x_after)
    x_after_far = far_x(1)
    twin(1, -1)
    twin(1, 1)
    wait(x_before_far)
    twin(-1, 2)
    landed(passing_table, 10)
    within_plane(passing_table, other_table, c, 9, 11)
    wait(other1)
    other2 = z_both(-2, 2, 1 - yl)
    wait(own4)
    cross4 = cross(4)
    wait(x_last)
    x_last_far = far_x(2)
    twin(2, -1)
    twin(2, 1)
    wait(x_after_far)
    twin(1, 2)
    wait(x_last_far)
    twin(2, 2)
    wait([cross4])
    wait(other2)
    wait(twins)

    def product(lhs, rhs):
        return jnp.dot(lhs, rhs, preferred_element_type=jnp.float32)

    def split(value):
        high = value.astype(jnp.bfloat16).astype(jnp.float32)
        return high, value - high

    landed(other_table, 11)
    high, low = split(other_table[...] - jnp.sum(other_table[...], axis=0, keepdims=True) / (2 * NT))
    nothing = jnp.zeros((1, LAG), jnp.float32)

    def three(value):
        return jnp.concatenate(
            [
                jnp.concatenate([value[:-1], nothing], axis=0),
                jnp.concatenate([value[1:], nothing], axis=0),
                jnp.concatenate([nothing, value[1:]], axis=0),
            ],
            axis=1,
        ).astype(jnp.bfloat16)

    high, low = three(high), three(low)
    right = jnp.concatenate([high, low, high], axis=0)
    for h in range(2):
        mine_high, mine_low = split(table[h] - jnp.sum(table[h], axis=0, keepdims=True) / (2 * NT))
        left = jnp.concatenate([mine_high, mine_high, mine_low], axis=0).T.astype(jnp.bfloat16)
        between = product(left, right) * LAG
        part = pl.ds(256 * h, 256)
        inst[part, :] = between[:, :LAG]
        lagged[part, :] = between[:, LAG : 2 * LAG]
        later[part, :] = between[:, 2 * LAG :]

    last = NT - 1
    head = rows[last, :, :LAG]
    middle[...] = product(rows[0, :, LAG:], cols[LAG : 2 * LAG, :]) + product(
        head, cols[512 * last : 512 * last + LAG, :]
    )
    lagged[...] += product(rows[0], cols[LAG : 3 * LAG, :])

    @pl.loop(1, NT - 1)
    def _(s):
        middle[...] += product(rows[s], cols[pl.ds(pl.multiple_of(s * 512, 512), 512), :])
        lagged[...] += product(rows[s], cols[pl.ds(pl.multiple_of(s * 512 + 256, 256), 512), :])

    lagged[...] += product(head, cols[512 * last + LAG :, :])
    inst[...] += middle[...] + product(rows[0, :, :LAG], cols[:LAG, :])
    later[...] += middle[...] + product(rows[last, :, LAG:], cols[512 * last + LAG :, :])

    for copy in sent:
        copy.wait_send()

    @pl.when(jnp.logical_not(in_plane))
    def _():
        for h in range(2):
            landed(halves.at[h], h)
        landed(passing_table, 8)

    for h in range(2):

        @pl.when(jnp.logical_not(jnp.logical_and(stays, c == h)))
        def _():
            landed(passing.at[h], 4 + h)

    @pl.when(jnp.logical_not(stays))
    def _():
        landed(passing_table, 9)


def on_device(frames):
    frame_count, panel = frames.shape
    block = jax.ShapeDtypeStruct((panel, frame_count), jnp.float32)
    vmem = pl.BlockSpec(memory_space=pltpu.VMEM)
    sums = pl.pallas_call(
        kernel,
        out_shape=(block, block, block),
        in_specs=[pl.BlockSpec(memory_space=pl.ANY)],
        out_specs=(vmem, vmem, vmem),
        scratch_shapes=[
            pltpu.VMEM((frame_count, panel), jnp.float32),
            pltpu.VMEM((2, frame_count, panel // 2), jnp.bfloat16),
            pltpu.VMEM((2, frame_count, panel // 2), jnp.bfloat16),
            pltpu.VMEM((2, NT, 8, 128), jnp.float32),
            pltpu.VMEM((2, 2 * NT, LAG), jnp.float32),
            pltpu.VMEM((2 * NT, LAG), jnp.float32),
            pltpu.VMEM((2 * NT, LAG), jnp.float32),
            pltpu.VMEM((panel, frame_count), jnp.float32),
            pltpu.VMEM((NT, panel, 2 * frame_count), jnp.bfloat16),
            pltpu.VMEM((NT * 2 * frame_count, panel // 2), jnp.bfloat16),
            pltpu.SemaphoreType.DMA,
            pltpu.SemaphoreType.DMA((N_COPIES,)),
            pltpu.SemaphoreType.DMA((N_COPIES,)),
            pltpu.SemaphoreType.DMA((12,)),
        ],
        compiler_params=pltpu.CompilerParams(
            collective_id=0, has_side_effects=True, vmem_limit_bytes=40 * 1024 * 1024
        ),
        cost_estimate=pl.CostEstimate(
            flops=4 * panel * frame_count * 8192, bytes_accessed=1 << 21, transcendentals=0
        ),
    )(frames)
    kept = LAG * (2 * NT - 1)
    return tuple(value / kept for value in sums)


def solution(mesh):
    return jax.shard_map(
        on_device,
        mesh=mesh,
        in_specs=(P("tm", "feat"),),
        out_specs=(P("feat", "tm"), P("feat", "tm"), P("feat", "tm")),
        check_vma=False,
    )
```

```python
import functools

import jax
import jax.numpy as jnp
from jax import lax
from jax.experimental import pallas as pl
from jax.experimental.pallas import tpu as pltpu
from jax.sharding import PartitionSpec as P

LAG = 256
MESH = pl.DeviceIdType.MESH

NYH, NX, NZ = 4, 4, 8
NT = NYH * NX
N_COPIES = 100


def mod(a, n):
    return lax.rem(a + n, n)


def kernel(
    x_hbm, inst, lagged, later, xv, halves, passing, means, table, passing_table, other_table, middle, rows, cols, in_sem, send_sem, recv_sem, turn_sem
):
    tm = lax.axis_index("tm")
    feat = lax.axis_index("feat")
    c = lax.rem(tm, 2)
    t = tm // 2
    yh, x = t // NX, lax.rem(t, NX)
    z, yl = feat // 2, lax.rem(feat, 2)
    p = feat
    def placed(yh, x, z, yl):
        odd = lax.rem(x, 2)
        steps = lax.rem(2 * lax.rem(x // 2 + x, 2) + lax.rem(yh // 2 + yh, 2) + 2 * yl, 4)
        return lax.rem((5 - 2 * odd) * z + 2 * steps + odd, NZ), lax.rem(yh, 2)

    odd = lax.rem(x, 2)
    factor = 5 - 2 * odd
    offset = lax.rem(placed(yh, x, 0, yl)[0], NZ)
    plane, side_to = placed(yh, x, z, yl)
    origin = lax.rem(factor * (z - offset + 2 * NZ), NZ)
    passed = 2 * origin + yl

    def block_at(z, side):
        z_from = t // 2
        low = lax.rem(z + z_from, 2)
        steps = lax.rem(z - (5 - 2 * low) * z_from - low + 8 * NZ, NZ) // 2
        steps = lax.rem(steps + 2 * lax.rem(t, 2), 4)
        return (2 * lax.rem(steps + side, 2) + side) * NX + 2 * lax.rem(steps // 2 + low, 2) + low

    mine = block_at(z, yl)
    in_plane = plane == z
    stays = jnp.logical_and(passed == t, side_to == yl)

    def device(dyh=0, dx=0, dz=0, core=c, yl=yl):
        return {
            "tm": (mod(yh + dyh, NYH) * NX + mod(x + dx, NX)) * 2 + core,
            "feat": mod(z + dz, NZ) * 2 + yl,
        }

    peers = [(a, b) for a in range(NYH) for b in range(NX) if a or b]

    barrier = pltpu.get_barrier_semaphore()
    load = pltpu.make_async_copy(x_hbm, xv, in_sem)
    load.start()
    near = [device(core=1 - c), device(dz=1), device(dz=-1), device(yl=1 - yl)]
    near += [device(dyh=a, dx=b) for a, b in peers]
    for who in near:
        pl.semaphore_signal(barrier, inc=1, device_id=who, device_id_type=MESH)

    @pl.when(jnp.logical_not(stays))
    def _():
        for h in range(2):
            pl.semaphore_signal(
                barrier, inc=1, device_id={"tm": 2 * mine + h, "feat": 2 * z + lax.rem(t, 2)}, device_id_type=MESH
            )

    ahead = {"tm": tm, "feat": 2 * plane + yl}

    @pl.when(jnp.logical_not(in_plane))
    def _():
        pl.semaphore_signal(
            barrier, inc=1, device_id={"tm": tm, "feat": passed}, device_id_type=MESH
        )

    load.wait()
    lanes = pl.ds(pl.multiple_of(c * LAG, LAG), LAG)
    block_mean = jnp.sum(xv[...], axis=0, keepdims=True) / LAG
    for k in range(4):
        mean = block_mean[:, 128 * k : 128 * (k + 1)]
        means[c, t, k : k + 1, :] = mean
        means[c, t, 4 + k : 5 + k, :] = mean
        part = (xv[:, 128 * k : 128 * (k + 1)] - mean).astype(jnp.bfloat16)
        halves[k // 2, :, 128 * (k % 2) : 128 * (k % 2 + 1)] = part
        rows[t, 128 * k : 128 * (k + 1), lanes] = part.T
    pl.semaphore_wait(barrier, len(near) + 3 - 2 * stays.astype(jnp.int32) - in_plane.astype(jnp.int32))

    sent = []

    def send(src, dst, who):
        k = len(sent)
        copy = pltpu.make_async_remote_copy(
            src_ref=src,
            dst_ref=dst,
            send_sem=send_sem.at[k],
            recv_sem=recv_sem.at[k],
            device_id=who,
            device_id_type=MESH,
        )
        copy.start()
        sent.append(copy)
        return copy

    def row(dyh, dx, half=None):
        s = mod(yh + dyh, NYH) * NX + mod(x + dx, NX)
        if half is None:
            return rows.at[s, :, lanes]
        return rows.at[s, pl.ds(256 * half, 256), lanes]

    def col(dz, side, half=None):
        s = block_at(mod(z + dz, NZ), side)
        if half is None:
            return cols.at[pl.ds(pl.multiple_of(s * 512, 512), 512), :]
        return cols.at[pl.ds(pl.multiple_of(s * 512 + 256 * half, 256), 256), :]

    def turned(half):
        return cols.at[pl.ds(pl.multiple_of(t * 512 + half * 256, 256), 256), :]

    def along_z(src, dst, k):
        copy = pltpu.make_async_remote_copy(
            src_ref=src,
            dst_ref=dst,
            send_sem=turn_sem.at[k],
            recv_sem=turn_sem.at[2 + k],
            device_id=ahead,
            device_id_type=MESH,
        )
        local = pltpu.make_async_copy(src, dst, turn_sem.at[2 + k])

        @pl.when(in_plane)
        def _():
            local.start()

        @pl.when(jnp.logical_not(in_plane))
        def _():
            copy.start()

    def within_plane(src, dst, h, send_k, recv_k):
        itself = jnp.logical_and(stays, c == h)
        copy = pltpu.make_async_remote_copy(
            src_ref=src,
            dst_ref=dst,
            send_sem=turn_sem.at[send_k],
            recv_sem=turn_sem.at[recv_k],
            device_id={"tm": 2 * passed + h, "feat": 2 * z + side_to},
            device_id_type=MESH,
        )
        local = pltpu.make_async_copy(src, dst, turn_sem.at[recv_k])

        @pl.when(itself)
        def _():
            local.start()

        @pl.when(jnp.logical_not(itself))
        def _():
            copy.start()

    def landed(ref, k):
        pltpu.make_async_copy(ref, ref, turn_sem.at[k]).wait()

    mean_arrivals = [send(means.at[c, t], means.at[c, t], device(dyh=a, dx=b)) for a, b in peers]
    for h in range(2):
        along_z(halves.at[h], passing.at[h], h)

    def turn(h):
        landed(passing.at[h], 2 + h)
        within_plane(passing.at[h], turned(c), h, 4 + h, 6 + c)

    def both(dyh, dx):
        return (
            send(row(dyh, dx), row(dyh, dx), device(dx=1)),
            send(row(dyh, dx), row(dyh, dx), device(dx=-1)),
        )

    def far_x(dyh):
        return (
            send(row(dyh, -1, 0), row(dyh, -1, 0), device(dx=1)),
            send(row(dyh, 1, 1), row(dyh, 1, 1), device(dx=-1)),
        )

    twins = []

    def twin(dyh, dx):
        twins.append(send(row(dyh, dx), row(dyh, dx), device(core=1 - c)))

    def wait(copies):
        for copy in copies:
            copy.wait_recv()

    def z_both(plus, minus, side, part):
        return (
            send(col(plus, side, part), col(plus, side, part), device(dz=1)),
            send(col(minus, side, part), col(minus, side, part), device(dz=-1)),
        )

    def cross(dz, part):
        return send(col(dz, yl, part), col(dz, yl, part), device(yl=1 - yl))

    y_near = (
        send(row(0, 0), row(0, 0), device(dyh=1)),
        send(row(0, 0), row(0, 0), device(dyh=-1)),
    )
    x_own = both(0, 0)
    twin(0, 0)

    wait(x_own)
    x_own_far = far_x(0)
    twin(0, -1)
    twin(0, 1)
    wait(mean_arrivals)
    mean_twin = send(means.at[c], means.at[c], device(core=1 - c))
    wait([mean_twin])
    for s in range(NT):
        for core in range(2):
            for k in range(4):
                line = 2 * s + core
                table[k // 2, line : line + 1, 128 * (k % 2) : 128 * (k % 2 + 1)] = means[core, s, k : k + 1, :]

    along_z(table.at[c], passing_table, 8)
    turn(0)
    turn(1)
    wait(y_near)
    y_far = (
        send(row(-1, 0, 0), row(-1, 0, 0), device(dyh=1)),
        send(row(1, 0, 1), row(1, 0, 1), device(dyh=-1)),
    )
    x_before = both(-1, 0)
    twin(-1, 0)
    twin(1, 0)
    x_after = both(1, 0)
    own1 = []
    for part in range(2):
        landed(passing.at[part], 6 + part)
        own1.append(z_both(0, 0, yl, part))
    cross0 = [cross(0, 0), cross(0, 1)]
    landed(passing_table, 10)
    within_plane(passing_table, other_table, c, 9, 11)

    wait(x_own_far)
    twin(0, 2)

    wait(x_before)
    x_before_far = far_x(-1)
    twin(-1, -1)
    twin(-1, 1)

    own2, cross1 = [], []
    for part in range(2):
        wait(own1[part])
        own2.append(z_both(-1, 1, yl, part))
    for part in range(2):
        cross1.append((cross(-1, part), cross(1, part)))

    wait(y_far)
    x_last = both(2, 0)
    twin(2, 0)

    wait(x_after)
    x_after_far = far_x(1)
    twin(1, -1)
    twin(1, 1)

    own3 = []
    for part in range(2):
        wait(own2[part])
        own3.append(z_both(-2, 2, yl, part))

    wait(cross0)
    other1 = []
    for part in range(2):
        wait(cross1[part])
        other1.append(z_both(-1, 1, 1 - yl, part))

    wait(x_last)
    x_last_far = far_x(2)
    twin(2, -1)
    twin(2, 1)

    wait(x_before_far)
    twin(-1, 2)

    wait(own3[0])
    wait(own3[1])
    own4 = (
        send(col(-3, yl, 0), col(-3, yl, 0), device(dz=1)),
        send(col(3, yl, 1), col(3, yl, 1), device(dz=-1)),
    )

    wait(x_after_far)
    twin(1, 2)

    other2 = []
    for part in range(2):
        wait(other1[part])
        other2.append(z_both(-2, 2, 1 - yl, part))

    cross4 = []
    for part in range(2):
        wait([own4[part]])
        cross4.append(cross(4, part))

    wait(x_last_far)
    twin(2, 2)

    def product(lhs, rhs):
        return jnp.dot(lhs, rhs, preferred_element_type=jnp.float32)

    def split(value):
        high = value.astype(jnp.bfloat16).astype(jnp.float32)
        return high, value - high

    landed(other_table, 11)
    high, low = split(other_table[...] - jnp.sum(other_table[...], axis=0, keepdims=True) / (2 * NT))
    nothing = jnp.zeros((1, LAG), jnp.float32)

    def three(value):
        return jnp.concatenate(
            [
                jnp.concatenate([value[:-1], nothing], axis=0),
                jnp.concatenate([value[1:], nothing], axis=0),
                jnp.concatenate([nothing, value[1:]], axis=0),
            ],
            axis=1,
        ).astype(jnp.bfloat16)

    high, low = three(high), three(low)
    right = jnp.concatenate([high, low, high], axis=0)
    for h in range(2):
        mine_high, mine_low = split(table[h] - jnp.sum(table[h], axis=0, keepdims=True) / (2 * NT))
        left = jnp.concatenate([mine_high, mine_high, mine_low], axis=0).T.astype(jnp.bfloat16)
        between = product(left, right) * LAG
        part = pl.ds(256 * h, 256)
        inst[part, :] = between[:, :LAG]
        lagged[part, :] = between[:, LAG : 2 * LAG]
        later[part, :] = between[:, 2 * LAG :]

    def col_here(s):
        where, side = placed(s // NX, lax.rem(s, NX), t // 2, lax.rem(t, 2))
        steps = mod(where - z, NZ)
        return jnp.logical_or(side == yl, jnp.logical_or(steps < 3, steps > 5))

    def multiply(first):
        @pl.loop(1, NT - 1)
        def _(s):
            both_here = col_here(s)
            next_here = jnp.logical_and(both_here, col_here(s + 1))

            @pl.when(both_here if first else jnp.logical_not(both_here))
            def _():
                middle[...] += product(rows[s], cols[pl.ds(pl.multiple_of(s * 512, 512), 512), :])

            @pl.when(next_here if first else jnp.logical_not(next_here))
            def _():
                lagged[...] += product(rows[s], cols[pl.ds(pl.multiple_of(s * 512 + 256, 256), 512), :])

    wait(twins)
    middle[...] = jnp.zeros_like(middle)
    multiply(True)

    wait(cross4)
    for part in range(2):
        wait(other2[part])
    multiply(False)

    last = NT - 1
    head = rows[last, :, :LAG]
    middle[...] += product(rows[0, :, LAG:], cols[LAG : 2 * LAG, :]) + product(
        head, cols[512 * last : 512 * last + LAG, :]
    )
    lagged[...] += product(rows[0], cols[LAG : 3 * LAG, :])
    lagged[...] += product(head, cols[512 * last + LAG :, :])
    inst[...] += middle[...] + product(rows[0, :, :LAG], cols[:LAG, :])
    later[...] += middle[...] + product(rows[last, :, LAG:], cols[512 * last + LAG :, :])

    for copy in sent:
        copy.wait_send()

    @pl.when(jnp.logical_not(in_plane))
    def _():
        for h in range(2):
            landed(halves.at[h], h)
        landed(passing_table, 8)

    for h in range(2):

        @pl.when(jnp.logical_not(jnp.logical_and(stays, c == h)))
        def _():
            landed(passing.at[h], 4 + h)

    @pl.when(jnp.logical_not(stays))
    def _():
        landed(passing_table, 9)


def on_device(frames):
    frame_count, panel = frames.shape
    block = jax.ShapeDtypeStruct((panel, frame_count), jnp.float32)
    vmem = pl.BlockSpec(memory_space=pltpu.VMEM)
    sums = pl.pallas_call(
        kernel,
        out_shape=(block, block, block),
        in_specs=[pl.BlockSpec(memory_space=pl.ANY)],
        out_specs=(vmem, vmem, vmem),
        scratch_shapes=[
            pltpu.VMEM((frame_count, panel), jnp.float32),
            pltpu.VMEM((2, frame_count, panel // 2), jnp.bfloat16),
            pltpu.VMEM((2, frame_count, panel // 2), jnp.bfloat16),
            pltpu.VMEM((2, NT, 8, 128), jnp.float32),
            pltpu.VMEM((2, 2 * NT, LAG), jnp.float32),
            pltpu.VMEM((2 * NT, LAG), jnp.float32),
            pltpu.VMEM((2 * NT, LAG), jnp.float32),
            pltpu.VMEM((panel, frame_count), jnp.float32),
            pltpu.VMEM((NT, panel, 2 * frame_count), jnp.bfloat16),
            pltpu.VMEM((NT * 2 * frame_count, panel // 2), jnp.bfloat16),
            pltpu.SemaphoreType.DMA,
            pltpu.SemaphoreType.DMA((N_COPIES,)),
            pltpu.SemaphoreType.DMA((N_COPIES,)),
            pltpu.SemaphoreType.DMA((12,)),
        ],
        compiler_params=pltpu.CompilerParams(
            collective_id=0, has_side_effects=True, vmem_limit_bytes=40 * 1024 * 1024
        ),
        cost_estimate=pl.CostEstimate(
            flops=4 * panel * frame_count * 8192, bytes_accessed=1 << 21, transcendentals=0
        ),
    )(frames)
    kept = LAG * (2 * NT - 1)
    return tuple(value / kept for value in sums)


def solution(mesh):
    return jax.shard_map(
        on_device,
        mesh=mesh,
        in_specs=(P("tm", "feat"),),
        out_specs=(P("feat", "tm"), P("feat", "tm"), P("feat", "tm")),
        check_vma=False,
    )
```

```python
import functools

import jax
import jax.numpy as jnp
from jax import lax
from jax.experimental import pallas as pl
from jax.experimental.pallas import tpu as pltpu
from jax.sharding import PartitionSpec as P

LAG = 256
MESH = pl.DeviceIdType.MESH

NYH, NX, NZ = 4, 4, 8
NT = NYH * NX
N_COPIES = 100


def mod(a, n):
    return lax.rem(a + n, n)


def kernel(
    x_hbm, inst, lagged, later, xv, halves, passing, means, table, passing_table, other_table, middle, rows, cols, in_sem, send_sem, recv_sem, turn_sem
):
    tm = lax.axis_index("tm")
    feat = lax.axis_index("feat")
    c = lax.rem(tm, 2)
    t = tm // 2
    yh, x = t // NX, lax.rem(t, NX)
    z, yl = feat // 2, lax.rem(feat, 2)
    p = feat
    def placed(yh, x, z, yl):
        odd = lax.rem(x, 2)
        steps = lax.rem(2 * lax.rem(x // 2 + x, 2) + lax.rem(yh // 2 + yh, 2) + 2 * yl, 4)
        return lax.rem((5 - 2 * odd) * z + 2 * steps + odd, NZ), lax.rem(yh, 2)

    odd = lax.rem(x, 2)
    factor = 5 - 2 * odd
    offset = lax.rem(placed(yh, x, 0, yl)[0], NZ)
    plane, side_to = placed(yh, x, z, yl)
    origin = lax.rem(factor * (z - offset + 2 * NZ), NZ)
    passed = 2 * origin + yl

    def block_at(z, side):
        z_from = t // 2
        low = lax.rem(z + z_from, 2)
        steps = lax.rem(z - (5 - 2 * low) * z_from - low + 8 * NZ, NZ) // 2
        steps = lax.rem(steps + 2 * lax.rem(t, 2), 4)
        return (2 * lax.rem(steps + side, 2) + side) * NX + 2 * lax.rem(steps // 2 + low, 2) + low

    mine = block_at(z, yl)
    in_plane = plane == z
    stays = jnp.logical_and(passed == t, side_to == yl)

    def device(dyh=0, dx=0, dz=0, core=c, yl=yl):
        return {
            "tm": (mod(yh + dyh, NYH) * NX + mod(x + dx, NX)) * 2 + core,
            "feat": mod(z + dz, NZ) * 2 + yl,
        }

    peers = [(a, b) for a in range(NYH) for b in range(NX) if a or b]

    barrier = pltpu.get_barrier_semaphore()
    load = pltpu.make_async_copy(x_hbm, xv, in_sem)
    load.start()
    near = [device(core=1 - c), device(dz=1), device(dz=-1), device(yl=1 - yl)]
    near += [device(dyh=a, dx=b) for a, b in peers]
    for who in near:
        pl.semaphore_signal(barrier, inc=1, device_id=who, device_id_type=MESH)

    @pl.when(jnp.logical_not(stays))
    def _():
        for h in range(2):
            pl.semaphore_signal(
                barrier, inc=1, device_id={"tm": 2 * mine + h, "feat": 2 * z + lax.rem(t, 2)}, device_id_type=MESH
            )

    ahead = {"tm": tm, "feat": 2 * plane + yl}

    @pl.when(jnp.logical_not(in_plane))
    def _():
        pl.semaphore_signal(
            barrier, inc=1, device_id={"tm": tm, "feat": passed}, device_id_type=MESH
        )

    load.wait()
    lanes = pl.ds(pl.multiple_of(c * LAG, LAG), LAG)
    block_mean = jnp.sum(xv[...], axis=0, keepdims=True) / LAG
    for k in range(4):
        mean = block_mean[:, 128 * k : 128 * (k + 1)]
        means[c, t, k : k + 1, :] = mean
        means[c, t, 4 + k : 5 + k, :] = mean
        part = (xv[:, 128 * k : 128 * (k + 1)] - mean).astype(jnp.bfloat16)
        halves[k // 2, :, 128 * (k % 2) : 128 * (k % 2 + 1)] = part
        rows[t, 128 * k : 128 * (k + 1), lanes] = part.T
    pl.semaphore_wait(barrier, len(near) + 3 - 2 * stays.astype(jnp.int32) - in_plane.astype(jnp.int32))

    sent = []

    def send(src, dst, who):
        k = len(sent)
        copy = pltpu.make_async_remote_copy(
            src_ref=src,
            dst_ref=dst,
            send_sem=send_sem.at[k],
            recv_sem=recv_sem.at[k],
            device_id=who,
            device_id_type=MESH,
        )
        copy.start()
        sent.append(copy)
        return copy

    def row(dyh, dx, half=None):
        s = mod(yh + dyh, NYH) * NX + mod(x + dx, NX)
        if half is None:
            return rows.at[s, :, lanes]
        return rows.at[s, pl.ds(256 * half, 256), lanes]

    def col(dz, side, half=None):
        s = block_at(mod(z + dz, NZ), side)
        if half is None:
            return cols.at[pl.ds(pl.multiple_of(s * 512, 512), 512), :]
        return cols.at[pl.ds(pl.multiple_of(s * 512 + 256 * half, 256), 256), :]

    def turned(half):
        return cols.at[pl.ds(pl.multiple_of(t * 512 + half * 256, 256), 256), :]

    def along_z(src, dst, k):
        copy = pltpu.make_async_remote_copy(
            src_ref=src,
            dst_ref=dst,
            send_sem=turn_sem.at[k],
            recv_sem=turn_sem.at[2 + k],
            device_id=ahead,
            device_id_type=MESH,
        )
        local = pltpu.make_async_copy(src, dst, turn_sem.at[2 + k])

        @pl.when(in_plane)
        def _():
            local.start()

        @pl.when(jnp.logical_not(in_plane))
        def _():
            copy.start()

    def within_plane(src, dst, h, send_k, recv_k):
        itself = jnp.logical_and(stays, c == h)
        copy = pltpu.make_async_remote_copy(
            src_ref=src,
            dst_ref=dst,
            send_sem=turn_sem.at[send_k],
            recv_sem=turn_sem.at[recv_k],
            device_id={"tm": 2 * passed + h, "feat": 2 * z + side_to},
            device_id_type=MESH,
        )
        local = pltpu.make_async_copy(src, dst, turn_sem.at[recv_k])

        @pl.when(itself)
        def _():
            local.start()

        @pl.when(jnp.logical_not(itself))
        def _():
            copy.start()

    def landed(ref, k):
        pltpu.make_async_copy(ref, ref, turn_sem.at[k]).wait()

    mean_arrivals = [send(means.at[c, t], means.at[c, t], device(dyh=a, dx=b)) for a, b in peers]
    for h in range(2):
        along_z(halves.at[h], passing.at[h], h)

    def turn(h):
        landed(passing.at[h], 2 + h)
        within_plane(passing.at[h], turned(c), h, 4 + h, 6 + c)

    def both(dyh, dx):
        return (
            send(row(dyh, dx), row(dyh, dx), device(dx=1)),
            send(row(dyh, dx), row(dyh, dx), device(dx=-1)),
        )

    def far_x(dyh):
        return (
            send(row(dyh, -1, 0), row(dyh, -1, 0), device(dx=1)),
            send(row(dyh, 1, 1), row(dyh, 1, 1), device(dx=-1)),
        )

    twins = []

    def twin(dyh, dx):
        twins.append(send(row(dyh, dx), row(dyh, dx), device(core=1 - c)))

    def wait(copies):
        for copy in copies:
            copy.wait_recv()

    def z_both(plus, minus, side, part):
        return (
            send(col(plus, side, part), col(plus, side, part), device(dz=1)),
            send(col(minus, side, part), col(minus, side, part), device(dz=-1)),
        )

    def cross(dz, part):
        return send(col(dz, yl, part), col(dz, yl, part), device(yl=1 - yl))

    x_own = both(0, 0)
    y_near = (
        send(row(0, 0), row(0, 0), device(dyh=1)),
        send(row(0, 0), row(0, 0), device(dyh=-1)),
    )
    twin(0, 0)

    wait(x_own)
    x_own_far = far_x(0)
    twin(0, -1)
    twin(0, 1)
    wait(mean_arrivals)
    mean_twin = send(means.at[c], means.at[c], device(core=1 - c))
    wait([mean_twin])
    for s in range(NT):
        for core in range(2):
            for k in range(4):
                line = 2 * s + core
                table[k // 2, line : line + 1, 128 * (k % 2) : 128 * (k % 2 + 1)] = means[core, s, k : k + 1, :]

    along_z(table.at[c], passing_table, 8)
    turn(0)
    turn(1)
    wait(y_near)
    y_far = (
        send(row(-1, 0, 0), row(-1, 0, 0), device(dyh=1)),
        send(row(1, 0, 1), row(1, 0, 1), device(dyh=-1)),
    )
    x_before = both(-1, 0)
    twin(-1, 0)
    twin(1, 0)
    x_after = both(1, 0)
    own1 = []
    for part in range(2):
        landed(passing.at[part], 6 + part)
        own1.append(z_both(0, 0, yl, part))
    cross0 = [cross(0, 0), cross(0, 1)]
    landed(passing_table, 10)
    within_plane(passing_table, other_table, c, 9, 11)

    wait(x_own_far)
    twin(0, 2)

    wait(x_before)
    x_before_far = far_x(-1)
    twin(-1, -1)
    twin(-1, 1)

    own2, cross1 = [], []
    for part in range(2):
        wait(own1[part])
        own2.append(z_both(-1, 1, yl, part))
    for part in range(2):
        cross1.append((cross(-1, part), cross(1, part)))

    wait(y_far)
    x_last = both(2, 0)
    twin(2, 0)

    wait(x_after)
    x_after_far = far_x(1)
    twin(1, -1)
    twin(1, 1)

    own3 = []
    for part in range(2):
        wait(own2[part])
        own3.append(z_both(-2, 2, yl, part))

    wait(cross0)
    other1 = []
    for part in range(2):
        wait(cross1[part])
        other1.append(z_both(-1, 1, 1 - yl, part))

    wait(x_last)
    x_last_far = far_x(2)
    twin(2, -1)
    twin(2, 1)

    wait(x_before_far)
    twin(-1, 2)

    wait(own3[0])
    wait(own3[1])
    own4 = (
        send(col(-3, yl, 0), col(-3, yl, 0), device(dz=1)),
        send(col(3, yl, 1), col(3, yl, 1), device(dz=-1)),
    )

    wait(x_after_far)
    twin(1, 2)

    other2 = []
    for part in range(2):
        wait(other1[part])
        other2.append(z_both(-2, 2, 1 - yl, part))

    cross4 = []
    for part in range(2):
        wait([own4[part]])
        cross4.append(cross(4, part))

    wait(x_last_far)
    twin(2, 2)

    def product(lhs, rhs):
        return jnp.dot(lhs, rhs, preferred_element_type=jnp.float32)

    def split(value):
        high = value.astype(jnp.bfloat16).astype(jnp.float32)
        return high, value - high

    landed(other_table, 11)
    high, low = split(other_table[...] - jnp.sum(other_table[...], axis=0, keepdims=True) / (2 * NT))
    nothing = jnp.zeros((1, LAG), jnp.float32)

    def three(value):
        return jnp.concatenate(
            [
                jnp.concatenate([value[:-1], nothing], axis=0),
                jnp.concatenate([value[1:], nothing], axis=0),
                jnp.concatenate([nothing, value[1:]], axis=0),
            ],
            axis=1,
        ).astype(jnp.bfloat16)

    high, low = three(high), three(low)
    right = jnp.concatenate([high, low, high], axis=0)
    for h in range(2):
        mine_high, mine_low = split(table[h] - jnp.sum(table[h], axis=0, keepdims=True) / (2 * NT))
        left = jnp.concatenate([mine_high, mine_high, mine_low], axis=0).T.astype(jnp.bfloat16)
        between = product(left, right) * LAG
        part = pl.ds(256 * h, 256)
        inst[part, :] = between[:, :LAG]
        lagged[part, :] = between[:, LAG : 2 * LAG]
        later[part, :] = between[:, 2 * LAG :]

    def col_here(s):
        where, side = placed(s // NX, lax.rem(s, NX), t // 2, lax.rem(t, 2))
        steps = mod(where - z, NZ)
        return jnp.logical_or(side == yl, jnp.logical_or(steps < 3, steps > 5))

    def multiply(first):
        @pl.loop(1, NT - 1)
        def _(s):
            both_here = col_here(s)
            next_here = jnp.logical_and(both_here, col_here(s + 1))

            @pl.when(both_here if first else jnp.logical_not(both_here))
            def _():
                middle[...] += product(rows[s], cols[pl.ds(pl.multiple_of(s * 512, 512), 512), :])

            @pl.when(next_here if first else jnp.logical_not(next_here))
            def _():
                lagged[...] += product(rows[s], cols[pl.ds(pl.multiple_of(s * 512 + 256, 256), 512), :])

    wait(twins)
    middle[...] = jnp.zeros_like(middle)
    multiply(True)

    wait(cross4)
    for part in range(2):
        wait(other2[part])
    multiply(False)

    last = NT - 1
    head = rows[last, :, :LAG]
    middle[...] += product(rows[0, :, LAG:], cols[LAG : 2 * LAG, :]) + product(
        head, cols[512 * last : 512 * last + LAG, :]
    )
    lagged[...] += product(rows[0], cols[LAG : 3 * LAG, :])
    lagged[...] += product(head, cols[512 * last + LAG :, :])
    inst[...] += middle[...] + product(rows[0, :, :LAG], cols[:LAG, :])
    later[...] += middle[...] + product(rows[last, :, LAG:], cols[512 * last + LAG :, :])

    for copy in sent:
        copy.wait_send()

    @pl.when(jnp.logical_not(in_plane))
    def _():
        for h in range(2):
            landed(halves.at[h], h)
        landed(passing_table, 8)

    for h in range(2):

        @pl.when(jnp.logical_not(jnp.logical_and(stays, c == h)))
        def _():
            landed(passing.at[h], 4 + h)

    @pl.when(jnp.logical_not(stays))
    def _():
        landed(passing_table, 9)


def on_device(frames):
    frame_count, panel = frames.shape
    block = jax.ShapeDtypeStruct((panel, frame_count), jnp.float32)
    vmem = pl.BlockSpec(memory_space=pltpu.VMEM)
    sums = pl.pallas_call(
        kernel,
        out_shape=(block, block, block),
        in_specs=[pl.BlockSpec(memory_space=pl.ANY)],
        out_specs=(vmem, vmem, vmem),
        scratch_shapes=[
            pltpu.VMEM((frame_count, panel), jnp.float32),
            pltpu.VMEM((2, frame_count, panel // 2), jnp.bfloat16),
            pltpu.VMEM((2, frame_count, panel // 2), jnp.bfloat16),
            pltpu.VMEM((2, NT, 8, 128), jnp.float32),
            pltpu.VMEM((2, 2 * NT, LAG), jnp.float32),
            pltpu.VMEM((2 * NT, LAG), jnp.float32),
            pltpu.VMEM((2 * NT, LAG), jnp.float32),
            pltpu.VMEM((panel, frame_count), jnp.float32),
            pltpu.VMEM((NT, panel, 2 * frame_count), jnp.bfloat16),
            pltpu.VMEM((NT * 2 * frame_count, panel // 2), jnp.bfloat16),
            pltpu.SemaphoreType.DMA,
            pltpu.SemaphoreType.DMA((N_COPIES,)),
            pltpu.SemaphoreType.DMA((N_COPIES,)),
            pltpu.SemaphoreType.DMA((12,)),
        ],
        compiler_params=pltpu.CompilerParams(
            collective_id=0, has_side_effects=True, vmem_limit_bytes=40 * 1024 * 1024
        ),
        cost_estimate=pl.CostEstimate(
            flops=4 * panel * frame_count * 8192, bytes_accessed=1 << 21, transcendentals=0
        ),
    )(frames)
    kept = LAG * (2 * NT - 1)
    return tuple(value / kept for value in sums)


def solution(mesh):
    return jax.shard_map(
        on_device,
        mesh=mesh,
        in_specs=(P("tm", "feat"),),
        out_specs=(P("feat", "tm"), P("feat", "tm"), P("feat", "tm")),
        check_vma=False,
    )
```
